32 devices in a mesh: row: 8 (over y, x, core), col: 4 (over z).
Axes of the slice: x: 2, y: 2, z: 4, core: 2. Of those that a mesh axis runs over, the one named last changes fastest.
Arguments:
- object_field: float32 [2, 2, 1024, 512], P(None, None, 'row', 'col'), may hold values from -6 to 6
- probe_field: float32 [2, 128, 128], replicated, may hold values from -6 to 6
- intensity: float32 [8, 4, 6, 128, 128], P('row', 'col'), may hold values from 0.25 to 4
- counts: int32 [8, 4], P('row', 'col'), may hold values from 2 to 6, as said below
- offsets: int32 [8, 4, 6, 2], P('row', 'col'), may hold values from 0 to 64, as said below
Outputs:
- updated_object: float32 [2, 2, 1024, 512], P(None, None, 'row', 'col')
The draws below stay inside these ranges and needn't reach their ends.
Inputs may be any that keep to these rules, and one draw needn't show every extreme that they name: `counts`: each tile has at least 2 and at most 6 live slots; some tile has exactly 6 and some exactly 2. `offsets`: offsets keep every window inside its bordered tile; both ends of the range occur in every draw.
All inputs are finite; a program needn't handle non-finite values.
Results may differ from the reference program's by a relative error of at most 0.0003.
Values sent between devices are 32-bit elements; how exact they have to be, the bound alone decides.
A program may use at most 64 MiB of HBM per device.

```python
import jax
import jax.numpy as jnp
from jax import lax

WIN = 128
BORDER = 32
MAXPOS = 6
SLICES = 2
ITERS = 2
TROWS = 8
TCOLS = 4
NR = 1024
NC = 512


def draw_counts(key, part):
    tile_count = TROWS * TCOLS
    values = jax.random.randint(key, (tile_count,), 2, MAXPOS + 1, dtype=jnp.int32)
    chosen = jax.random.permutation(jax.random.fold_in(key, 11), tile_count)
    values = values.at[chosen[0]].set(MAXPOS).at[chosen[1]].set(2)
    return values.reshape(TROWS, TCOLS)


def draw_offsets(key, part):
    full_shape = (TROWS, TCOLS, MAXPOS, 2)
    values = jax.random.randint(key, full_shape, 0, 2 * BORDER + 1, dtype=jnp.int32)
    flattened = values.reshape(-1)
    chosen = jax.random.permutation(jax.random.fold_in(key, 13), flattened.shape[0])
    flattened = flattened.at[chosen[0]].set(2 * BORDER).at[chosen[1]].set(0)
    return flattened.reshape(full_shape)


def block_scale(stream_key, extent, cuts, least, largest):
    level, own = 1.0, jax.random.fold_in(stream_key, 6)
    for dim, parts in cuts:
        draws = jnp.exp(jax.random.uniform(jax.random.fold_in(own, dim), (parts,), jnp.float32, least / len(cuts), largest / len(cuts)))
        level = level * jnp.repeat(draws, extent[dim] // parts).reshape([-1 if axis == dim else 1 for axis in range(len(extent))])
    return level


def bell_draw(rng, extent, scale, reach, shards=(), held_as=jnp.bfloat16):
    level = block_scale(rng, extent, shards, -0.22, 0.18) if shards else 1.0
    entries = jax.random.normal(rng, extent, jnp.float32) * scale * level
    return jnp.minimum(jnp.maximum(entries, -reach), reach).astype(held_as)


def setup_inputs(seed: int = 0) -> dict:
    key_of = jax.random.split(jax.random.key(seed), 6)
    return {
        "object_field": bell_draw(key_of[0], (SLICES, 2, NR, NC), 1.0, 6.0, ((2, 8), (3, 4)), jnp.float32),
        "probe_field": bell_draw(key_of[1], (2, WIN, WIN), 1.0, 6.0, (), jnp.float32),
        "intensity": jnp.clip(0.25 + 3.75 * jax.random.uniform(key_of[2], (TROWS, TCOLS, MAXPOS, WIN, WIN), jnp.float32) ** block_scale(key_of[2], (TROWS, TCOLS, MAXPOS, WIN, WIN), ((0, 8), (1, 4)), -0.2, 0.2), 0.25, 4.0),
        "counts": draw_counts(jax.random.fold_in(key_of[5], 71), 0),
        "offsets": draw_offsets(jax.random.fold_in(key_of[5], 71), 0),
    }


step_size = 0.25
chirp = 0.7
highest = lax.Precision.HIGHEST

def conjugate(values):
    return jnp.stack([values[..., 0, :, :], -values[..., 1, :, :]], axis=-3)

def complex_product(first, second):
    real_part = first[..., 0, :, :] * second[..., 0, :, :] - first[..., 1, :, :] * second[..., 1, :, :]
    imag_part = first[..., 0, :, :] * second[..., 1, :, :] + first[..., 1, :, :] * second[..., 0, :, :]
    return jnp.stack([real_part, imag_part], axis=-3)

def multiply_left(matrix, values):
    return jnp.einsum('ij,...jk->...ik', matrix, values, precision=highest)

def multiply_right(values, matrix):
    return jnp.einsum('...ij,jk->...ik', values, matrix, precision=highest)

def apply_left(matrix, values):
    real_part = multiply_left(matrix[0], values[..., 0, :, :]) - multiply_left(matrix[1], values[..., 1, :, :])
    imag_part = multiply_left(matrix[0], values[..., 1, :, :]) + multiply_left(matrix[1], values[..., 0, :, :])
    return jnp.stack([real_part, imag_part], axis=-3)

def apply_right(values, matrix):
    real_part = multiply_right(values[..., 0, :, :], matrix[0]) - multiply_right(values[..., 1, :, :], matrix[1])
    imag_part = multiply_right(values[..., 0, :, :], matrix[1]) + multiply_right(values[..., 1, :, :], matrix[0])
    return jnp.stack([real_part, imag_part], axis=-3)

def transposed(values):
    return jnp.swapaxes(values, -1, -2)

def fourier_tables(window_size):
    positions = jnp.arange(window_size, dtype=jnp.int32)
    products = positions[:, None] * positions[None, :] % window_size
    angles = -2.0 * jnp.pi / window_size * products.astype(jnp.float32)
    norm_factor = 1.0 / jnp.sqrt(jnp.float32(window_size))
    fourier = jnp.stack([jnp.cos(angles), jnp.sin(angles)]) * norm_factor
    frequency = jnp.where(positions < window_size // 2, positions, positions - window_size).astype(jnp.float32)
    phases = chirp * jnp.pi / window_size * frequency * frequency
    kernel = jnp.stack([jnp.cos(phases), -jnp.sin(phases)])[:, :, None]
    propagator = apply_left(conjugate(fourier), complex_product(kernel, fourier))
    return (fourier, propagator)

def slot_gradients(probe_field, first_slice, second_slice, amplitude, fourier, propagator):
    incident = complex_product(probe_field, first_slice)
    propagated = apply_right(apply_left(propagator, incident), transposed(propagator))
    exit_wave = complex_product(propagated, second_slice)
    far_field = apply_right(apply_left(fourier, exit_wave), fourier)
    magnitude = jnp.sqrt(far_field[:, 0] * far_field[:, 0] + far_field[:, 1] * far_field[:, 1] + 1.0)
    residual = far_field * (1.0 - amplitude / magnitude)[:, None]
    back_far = apply_right(apply_left(conjugate(fourier), residual), conjugate(fourier))
    grad_second = complex_product(conjugate(propagated), back_far)
    back_wave = complex_product(conjugate(second_slice), back_far)
    back_prop = apply_right(apply_left(transposed(conjugate(propagator)), back_wave), conjugate(propagator))
    grad_first = complex_product(conjugate(probe_field), back_prop)
    return (grad_first, grad_second)

def tile_gradients(bordered, probe_field, intensity, live_count, offsets, fourier, propagator):
    window_size = probe_field.shape[-1]
    slot_total = offsets.shape[0]
    zero_index = jnp.zeros((), jnp.int32)
    corners = [(zero_index, zero_index, offsets[slot_index, 0].astype(jnp.int32), offsets[slot_index, 1].astype(jnp.int32)) for slot_index in range(slot_total)]
    window_shape = (bordered.shape[0], 2, window_size, window_size)
    windows = jnp.stack([lax.dynamic_slice(bordered, corner_at, window_shape) for corner_at in corners])
    grad_first, grad_second = slot_gradients(probe_field, windows[:, 0], windows[:, 1], jnp.sqrt(intensity), fourier, propagator)
    live_mask = (jnp.arange(slot_total, dtype=jnp.int32) < live_count).astype(jnp.float32)[:, None, None, None, None]
    gradients = jnp.stack([grad_first, grad_second], axis=1) * live_mask
    accumulated = jnp.zeros_like(bordered)
    for slot_index in range(slot_total):
        current = lax.dynamic_slice(accumulated, corners[slot_index], window_shape)
        accumulated = lax.dynamic_update_slice(accumulated, current + gradients[slot_index], corners[slot_index])
    return accumulated

def reference(object_field, probe_field, intensity, counts, offsets):
    fourier, propagator = fourier_tables(WIN)
    bordered_size = WIN + 2 * BORDER
    pad_widths = ((0, 0), (0, 0), (BORDER, BORDER), (BORDER, BORDER))
    padded = jnp.pad(object_field, pad_widths)
    for sweep in range(ITERS):

        def device_step(accumulated, device_index, padded=padded):
            row_index = device_index // TCOLS
            col_index = device_index % TCOLS
            zero_index = jnp.zeros((), jnp.int32)
            corner_at = (zero_index, zero_index, (row_index * WIN).astype(jnp.int32), (col_index * WIN).astype(jnp.int32))
            bordered = lax.dynamic_slice(padded, corner_at, (SLICES, 2, bordered_size, bordered_size))
            gradients = tile_gradients(bordered, probe_field, intensity[row_index, col_index], counts[row_index, col_index], offsets[row_index, col_index], fourier, propagator)
            current = lax.dynamic_slice(accumulated, corner_at, gradients.shape)
            return (lax.dynamic_update_slice(accumulated, current + gradients, corner_at), None)
        accumulated, ignored = lax.scan(device_step, jnp.zeros_like(padded), jnp.arange(TROWS * TCOLS, dtype=jnp.int32))
        interior = (padded - step_size * accumulated)[:, :, BORDER:BORDER + NR, BORDER:BORDER + NC]
        padded = jnp.pad(interior, pad_widths)
    return padded[:, :, BORDER:BORDER + NR, BORDER:BORDER + NC]
```

```python
import functools

import jax
import jax.numpy as jnp
import ml_dtypes
import numpy as np
from jax import lax
from jax.experimental import pallas as pl
from jax.experimental.pallas import tpu as pltpu
from jax.sharding import PartitionSpec as P

BORDER = 32
ITERS = 2
STEP = 0.25
CHIRP = 0.7
DIRS = ((-1, 0), (1, 0), (0, -1), (0, 1), (-1, -1), (-1, 1), (1, -1), (1, 1))
BF = jnp.bfloat16
F32 = jnp.float32
MESH = pl.DeviceIdType.MESH


def tables(n):
    k = np.arange(n)
    ang = -2.0 * np.pi / n * ((k[:, None] * k[None, :]) % n)
    fourier = np.exp(1j * ang) / np.sqrt(n)
    freq = np.where(k < n // 2, k, k - n).astype(np.float64)
    kern = np.exp(-1j * CHIRP * np.pi / n * freq * freq)
    prop = fourier.conj() @ (kern[:, None] * fourier)
    prop = (prop + prop.T) / 2
    left, right = [], []
    for m in (prop, fourier, fourier.conj(), prop.conj()):
        lm = np.block([[m.real, -m.imag], [m.imag, m.real]])
        rm = np.block([[m.real, m.imag], [-m.imag, m.real]])
        for mat, out, axis in ((lm, left, 1), (rm, right, 0)):
            hi = mat.astype(np.float32).astype(ml_dtypes.bfloat16)
            lo = (mat - hi.astype(np.float64)).astype(np.float32).astype(ml_dtypes.bfloat16)
            out.append(np.concatenate([hi, hi, lo], axis=axis))
    return np.stack(left), np.stack(right)


def kernel(nr, nc, obj, probe, inten, counts, offs, lefts, rights, out,
           bord, amp, prop, win2, xc, xr, zb, gpad, acc, core,
           s_ud, s_lr, s_co, r_ud, r_lr, r_co, send_sem, recv_sem):
    n = probe.shape[-1]
    b = BORDER
    slots = inten.shape[0]
    ext = n + 2 * b
    me_r, me_c = lax.axis_index("row"), lax.axis_index("col")
    lane_group = lax.broadcasted_iota(jnp.int32, (1, n), 1) // b

    def exists(dr, dc):
        ok = None
        for pos, step, count in ((me_r, dr, nr), (me_c, dc, nc)):
            if step:
                cond = (pos > 0) if step < 0 else (pos < count - 1)
                ok = cond if ok is None else jnp.logical_and(ok, cond)
        return ok

    def bufs(phase, d):
        if d < 2:
            return s_ud.at[phase, d], r_ud.at[phase, d]
        if d < 4:
            return s_lr.at[phase, d - 2], r_lr.at[phase, d - 2]
        return s_co.at[phase, d - 4], r_co.at[phase, d - 4]

    def message(phase, d):
        src, dst = bufs(phase, d)
        dr, dc = DIRS[d]
        return pltpu.make_async_remote_copy(
            src_ref=src, dst_ref=dst,
            send_sem=send_sem.at[phase, d], recv_sem=recv_sem.at[phase, d],
            device_id=(me_r + dr, me_c + dc), device_id_type=MESH)

    def send(phase):
        for d in (2, 3, 4, 5, 6, 7, 0, 1):
            pl.when(exists(*DIRS[d]))(lambda d=d: message(phase, d).start())

    def wait_recv(phase):
        for d, (dr, dc) in enumerate(DIRS):
            pl.when(exists(-dr, -dc))(lambda d=d: message(phase, d).wait_recv())

    def wait_send(phase):
        for d, (dr, dc) in enumerate(DIRS):
            pl.when(exists(dr, dc))(lambda d=d: message(phase, d).wait_send())

    def pack(take, lane0, row0, rows):
        half = rows // 2
        total = None
        for g in range(4):
            piece = take(g // 2, row0 + (g % 2) * half, half)
            shift = (b * g - lane0) % n
            if shift:
                piece = pltpu.roll(piece, shift, 1)
            total = piece if total is None else jnp.where(lane_group == g, piece, total)
        return total

    def unpack(msg, g, lane0):
        shift = (lane0 - b * g) % n
        return pltpu.roll(msg, shift, 1) if shift else msg

    def pair(left_msg, right_msg, g, left_lane, right_lane):
        zero = jnp.zeros_like(left_msg)
        return jnp.where(lane_group == left_lane // b, unpack(left_msg, g, left_lane),
                         jnp.where(lane_group == right_lane // b,
                                   unpack(right_msg, g, right_lane), zero))

    def send_halo(phase, take):
        for ch in range(2):
            s_ud[phase, 0, ch] = take(ch, 0, b)
            s_ud[phase, 1, ch] = take(ch, n - b, b)
        for i, lane in enumerate((0, n - b)):
            s_lr[phase, i] = pack(take, lane, 0, n)
            s_co[phase, i] = pack(take, lane, 0, b)
            s_co[phase, 2 + i] = pack(take, lane, n - b, b)
        send(phase)

    def recv_halo(phase, sl):
        wait_recv(phase)
        for ch in range(2):
            k = 2 * sl + ch
            bord[k, 0, 0:b] = r_ud[phase, 1, ch]
            bord[k, 0, n + b:ext] = r_ud[phase, 0, ch]
            for h in range(2):
                g = 2 * ch + h
                row = b + h * (n // 2)
                bord[k, 1, row:row + n // 2] = pair(
                    r_lr[phase, 1], r_lr[phase, 0], g, n - b, 0)
                row = h * (b // 2)
                bord[k, 1, row:row + b // 2] = pair(
                    r_co[phase, 3], r_co[phase, 2], g, n - b, 0)
                row = n + b + h * (b // 2)
                bord[k, 1, row:row + b // 2] = pair(
                    r_co[phase, 1], r_co[phase, 0], g, n - b, 0)

    def send_rims(phase, it, sl):
        def take(ch, row, rows):
            return acc[it, sl, ch, 1, row:row + rows]
        for ch in range(2):
            s_ud[phase, 0, ch] = acc[it, sl, ch, 0, 0:b]
            s_ud[phase, 1, ch] = acc[it, sl, ch, 0, n + b:ext]
        for i, lane in enumerate((n - b, 0)):
            s_lr[phase, i] = pack(take, lane, b, n)
            s_co[phase, i] = pack(take, lane, 0, b)
            s_co[phase, 2 + i] = pack(take, lane, n + b, b)
        send(phase)

    def fold(phase, it, sl):
        wait_recv(phase)
        for ch in range(2):
            for h in range(2):
                g = 2 * ch + h
                row = h * (n // 2)
                core[ch, row:row + n // 2] = acc[it, sl, ch, 0, b + row:b + row + n // 2] + pair(
                    r_lr[phase, 1], r_lr[phase, 0], g, 0, n - b)
            core[ch, 0:b] = core[ch, 0:b] + r_ud[phase, 1, ch]
            core[ch, n - b:n] = core[ch, n - b:n] + r_ud[phase, 0, ch]
            for h in range(2):
                g = 2 * ch + h
                row = h * (b // 2)
                core[ch, row:row + b // 2] = core[ch, row:row + b // 2] + pair(
                    r_co[phase, 3], r_co[phase, 2], g, 0, n - b)
                row = n - b + h * (b // 2)
                core[ch, row:row + b // 2] = core[ch, row:row + b // 2] + pair(
                    r_co[phase, 1], r_co[phase, 0], g, 0, n - b)
        for ch in range(2):
            k = 2 * sl + ch
            new = bord[k, 0, b:b + n] - STEP * core[ch]
            if it == ITERS - 1:
                out[sl, ch] = new
            else:
                bord[k, 0, b:b + n] = new

    def parts(x):
        hi = x.astype(BF)
        return hi, (x - hi.astype(F32)).astype(BF)

    def put_col(s, re, im):
        cols = slice(s * n, (s + 1) * n)
        for i, x in enumerate((re, im)):
            hi, lo = parts(x)
            xc[i * n:(i + 1) * n, cols] = hi
            xc[(2 + i) * n:(3 + i) * n, cols] = lo
            xc[(4 + i) * n:(5 + i) * n, cols] = hi

    def transform(t):
        for p in range(slots // 2):
            y = jnp.dot(lefts[t], xc[:, 2 * p * n:2 * (p + 1) * n], preferred_element_type=F32)
            for q in range(2):
                s = 2 * p + q
                rows = slice(s * n, (s + 1) * n)
                for i in range(2):
                    hi, lo = parts(y[i * n:(i + 1) * n, q * n:(q + 1) * n])
                    xr[rows, i * n:(i + 1) * n] = hi
                    xr[rows, (2 + i) * n:(3 + i) * n] = lo
                    xr[rows, (4 + i) * n:(5 + i) * n] = hi
        zb[...] = jnp.dot(xr[...], rights[t], preferred_element_type=F32)

    def result(s):
        return zb[s * n:(s + 1) * n, 0:n], zb[s * n:(s + 1) * n, n:2 * n]

    def window(s, k):
        row, col = offs[0, 0, s, 0], offs[0, 0, s, 1]
        strip = jnp.concatenate([bord[k, h, pl.ds(row, n), :] for h in range(2)], axis=1)
        shift = lax.rem(2 * n + b - col, 2 * n)
        return pltpu.roll(strip, shift, 1)[:, 0:n]

    def place(s, ch, g):
        shift = lax.rem(2 * n - b + offs[0, 0, s, 1], 2 * n)
        wide = jnp.concatenate([g, jnp.zeros_like(g)], axis=1)
        wide = pltpu.roll(wide, shift, 1)
        for h in range(2):
            gpad[s, ch, h, 2 * b:2 * b + n] = wide[:, h * n:(h + 1) * n]

    def gather(it, sl):
        for ch in range(2):
            for h in range(2):
                total = None
                for s in range(slots):
                    term = gpad[s, ch, h, pl.ds(2 * b - offs[0, 0, s, 0], ext), :]
                    total = term if total is None else total + term
                acc[it, sl, ch, h] = total

    for buf in (r_ud, r_lr, r_co):
        buf[...] = jnp.zeros(buf.shape, F32)
    barrier = pltpu.get_barrier_semaphore()
    for dr, dc in DIRS:
        @pl.when(exists(dr, dc))
        def _(dr=dr, dc=dc):
            pl.semaphore_signal(barrier, inc=1, device_id=(me_r + dr, me_c + dc),
                                device_id_type=MESH)
    for s in range(slots):
        amp[s] = jnp.sqrt(inten[s])
        for ch in range(2):
            for h in range(2):
                gpad[s, ch, h, 0:2 * b] = jnp.zeros((2 * b, n), F32)
                gpad[s, ch, h, 2 * b + n:] = jnp.zeros((2 * b, n), F32)
    peers = sum(exists(dr, dc).astype(jnp.int32) for dr, dc in DIRS)
    pl.semaphore_wait(barrier, peers)
    for sl in range(2):
        send_halo(sl, lambda ch, row, rows, sl=sl: obj[sl, ch, row:row + rows, :])
    for sl in range(2):
        for ch in range(2):
            bord[2 * sl + ch, 0, b:b + n] = obj[sl, ch]

    live = counts[0, 0]
    pr, pi = probe.at[0], probe.at[1]
    halo = (0, 1)
    for it in range(ITERS):
        recv_halo(halo[0], 0)
        for s in range(slots):
            ar, ai = window(s, 0), window(s, 1)
            put_col(s, pr[...] * ar - pi[...] * ai, pr[...] * ai + pi[...] * ar)
        transform(0)
        recv_halo(halo[1], 1)
        for s in range(slots):
            ur, ui = result(s)
            ar, ai = window(s, 2), window(s, 3)
            prop[s, 0], prop[s, 1] = ur, ui
            win2[s, 0], win2[s, 1] = ar, ai
            put_col(s, ur * ar - ui * ai, ur * ai + ui * ar)
        transform(1)
        for s in range(slots):
            fr, fi = result(s)
            scale = 1.0 - amp[s] * lax.rsqrt(fr * fr + fi * fi + 1.0)
            scale = scale * (s < live).astype(F32)
            put_col(s, fr * scale, fi * scale)
        transform(2)
        for s in range(slots):
            br, bi = result(s)
            ur, ui = prop[s, 0], prop[s, 1]
            ar, ai = win2[s, 0], win2[s, 1]
            place(s, 0, ur * br + ui * bi)
            place(s, 1, ur * bi - ui * br)
            put_col(s, ar * br + ai * bi, ar * bi - ai * br)
        base = 2 + 4 * it
        gather(it, 1)
        send_rims(base, it, 1)
        transform(3)
        for s in range(slots):
            br, bi = result(s)
            place(s, 0, pr[...] * br + pi[...] * bi)
            place(s, 1, pr[...] * bi - pi[...] * br)
        gather(it, 0)
        send_rims(base + 1, it, 0)
        fold(base, it, 1)
        last = it == ITERS - 1
        if not last:
            send_halo(base + 2, lambda ch, row, rows: bord[2 + ch, 0, b + row:b + row + rows])
        fold(base + 1, it, 0)
        if not last:
            send_halo(base + 3, lambda ch, row, rows: bord[ch, 0, b + row:b + row + rows])
            halo = (base + 3, base + 2)
    for phase in range(4 * ITERS):
        wait_send(phase)


def local(nr, nc, object_field, probe_field, intensity, counts, offsets):
    n = object_field.shape[-1]
    b = BORDER
    slots = intensity.shape[2]
    ext = n + 2 * b
    lefts, rights = tables(n)
    phases = 4 * ITERS
    vmem = pl.BlockSpec(memory_space=pltpu.VMEM)
    smem = pl.BlockSpec(memory_space=pltpu.SMEM)
    messages = [
        pltpu.VMEM((phases, 2, 2, b, n), F32),
        pltpu.VMEM((phases, 2, n // 2, n), F32),
        pltpu.VMEM((phases, 4, b // 2, n), F32),
    ]
    return pl.pallas_call(
        functools.partial(kernel, nr, nc),
        out_shape=jax.ShapeDtypeStruct(object_field.shape, F32),
        in_specs=[vmem, vmem, vmem, smem, smem, vmem, vmem],
        out_specs=vmem,
        scratch_shapes=[
            pltpu.VMEM((4, 2, ext, n), F32),
            pltpu.VMEM((slots, n, n), F32),
            pltpu.VMEM((slots, 2, n, n), F32),
            pltpu.VMEM((slots, 2, n, n), F32),
            pltpu.VMEM((6 * n, slots * n), BF),
            pltpu.VMEM((slots * n, 6 * n), BF),
            pltpu.VMEM((slots * n, 2 * n), F32),
            pltpu.VMEM((slots, 2, 2, n + 4 * b, n), F32),
            pltpu.VMEM((ITERS, 2, 2, 2, ext, n), F32),
            pltpu.VMEM((2, n, n), F32),
            *messages,
            *messages,
            pltpu.SemaphoreType.DMA((phases, 8)),
            pltpu.SemaphoreType.DMA((phases, 8)),
        ],
        compiler_params=pltpu.CompilerParams(
            collective_id=0, has_side_effects=True, vmem_limit_bytes=40 * 1024 * 1024),
    )(object_field, probe_field, intensity[0, 0], counts, offsets,
      jnp.asarray(lefts), jnp.asarray(rights))


def solution(mesh):
    in_specs = (
        P(None, None, "row", "col"),
        P(),
        P("row", "col", None, None, None),
        P("row", "col"),
        P("row", "col", None, None),
    )
    out_specs = P(None, None, "row", "col")
    step = functools.partial(local, mesh.shape["row"], mesh.shape["col"])
    return jax.shard_map(step, mesh=mesh, in_specs=in_specs, out_specs=out_specs, check_vma=False)
```

```python
import functools

import jax
import jax.numpy as jnp
import ml_dtypes
import numpy as np
from jax import lax
from jax.experimental import pallas as pl
from jax.experimental.pallas import tpu as pltpu
from jax.sharding import PartitionSpec as P

BORDER = 32
ITERS = 2
STEP = 0.25
CHIRP = 0.7
DIRS = ((-1, 0), (1, 0), (0, -1), (0, 1), (-1, -1), (-1, 1), (1, -1), (1, 1))
BF = jnp.bfloat16
F32 = jnp.float32
MESH = pl.DeviceIdType.MESH


def tables(n):
    k = np.arange(n)
    ang = -2.0 * np.pi / n * ((k[:, None] * k[None, :]) % n)
    fourier = np.exp(1j * ang) / np.sqrt(n)
    freq = np.where(k < n // 2, k, k - n).astype(np.float64)
    kern = np.exp(-1j * CHIRP * np.pi / n * freq * freq)
    prop = fourier.conj() @ (kern[:, None] * fourier)
    prop = (prop + prop.T) / 2
    left, right = [], []
    for m in (prop, fourier, fourier.conj(), prop.conj()):
        lm = np.block([[m.real, -m.imag], [m.imag, m.real]])
        rm = np.block([[m.real, m.imag], [-m.imag, m.real]])
        for mat, out, axis in ((lm, left, 1), (rm, right, 0)):
            hi = mat.astype(np.float32).astype(ml_dtypes.bfloat16)
            lo = (mat - hi.astype(np.float64)).astype(np.float32).astype(ml_dtypes.bfloat16)
            out.append(np.concatenate([hi, hi, lo], axis=axis))
    return np.stack(left), np.stack(right)


def kernel(nr, nc, obj_h, probe_h, inten_h, counts, offs, lefts_h, rights_h, out,
           obj, probe, inten, lefts, rights, in_sem, yb, bord, amp, prop, win2, xc, xr, zb, gpad, acc, core,
           s_ud, s_lr, s_co, r_ud, r_lr, r_co, send_sem, recv_sem):
    n = probe.shape[-1]
    b = BORDER
    slots = inten.shape[0]
    ext = n + 2 * b
    me_r, me_c = lax.axis_index("row"), lax.axis_index("col")
    lane_group = lax.broadcasted_iota(jnp.int32, (1, n), 1) // b

    def exists(dr, dc):
        ok = None
        for pos, step, count in ((me_r, dr, nr), (me_c, dc, nc)):
            if step:
                cond = (pos > 0) if step < 0 else (pos < count - 1)
                ok = cond if ok is None else jnp.logical_and(ok, cond)
        return ok

    def bufs(phase, d):
        if d < 2:
            return s_ud.at[phase, d], r_ud.at[phase, d]
        if d < 4:
            return s_lr.at[phase, d - 2], r_lr.at[phase, d - 2]
        return s_co.at[phase, d - 4], r_co.at[phase, d - 4]

    def message(phase, d):
        src, dst = bufs(phase, d)
        dr, dc = DIRS[d]
        return pltpu.make_async_remote_copy(
            src_ref=src, dst_ref=dst,
            send_sem=send_sem.at[phase, d], recv_sem=recv_sem.at[phase, d],
            device_id=(me_r + dr, me_c + dc), device_id_type=MESH)

    def send(phase):
        for d in (2, 3, 4, 5, 6, 7, 0, 1):
            pl.when(exists(*DIRS[d]))(lambda d=d: message(phase, d).start())

    def wait_recv(phase):
        for d, (dr, dc) in enumerate(DIRS):
            pl.when(exists(-dr, -dc))(lambda d=d: message(phase, d).wait_recv())

    def wait_send(phase):
        for d, (dr, dc) in enumerate(DIRS):
            pl.when(exists(dr, dc))(lambda d=d: message(phase, d).wait_send())

    def pack(take, lane0, row0, rows):
        half = rows // 2
        total = None
        for g in range(4):
            piece = take(g // 2, row0 + (g % 2) * half, half)
            shift = (b * g - lane0) % n
            if shift:
                piece = pltpu.roll(piece, shift, 1)
            total = piece if total is None else jnp.where(lane_group == g, piece, total)
        return total

    def unpack(msg, g, lane0):
        shift = (lane0 - b * g) % n
        return pltpu.roll(msg, shift, 1) if shift else msg

    def pair(left_msg, right_msg, g, left_lane, right_lane):
        zero = jnp.zeros_like(left_msg)
        return jnp.where(lane_group == left_lane // b, unpack(left_msg, g, left_lane),
                         jnp.where(lane_group == right_lane // b,
                                   unpack(right_msg, g, right_lane), zero))

    def send_halo(phase, take):
        for ch in range(2):
            s_ud[phase, 0, ch] = take(ch, 0, b)
            s_ud[phase, 1, ch] = take(ch, n - b, b)
        for i, lane in enumerate((0, n - b)):
            s_lr[phase, i] = pack(take, lane, 0, n)
            s_co[phase, i] = pack(take, lane, 0, b)
            s_co[phase, 2 + i] = pack(take, lane, n - b, b)
        send(phase)

    def recv_halo(phase, sl):
        wait_recv(phase)
        for ch in range(2):
            k = 2 * sl + ch
            bord[k, 0, 0:b] = r_ud[phase, 1, ch]
            bord[k, 0, n + b:ext] = r_ud[phase, 0, ch]
            for h in range(2):
                g = 2 * ch + h
                row = b + h * (n // 2)
                bord[k, 1, row:row + n // 2] = pair(
                    r_lr[phase, 1], r_lr[phase, 0], g, n - b, 0)
                row = h * (b // 2)
                bord[k, 1, row:row + b // 2] = pair(
                    r_co[phase, 3], r_co[phase, 2], g, n - b, 0)
                row = n + b + h * (b // 2)
                bord[k, 1, row:row + b // 2] = pair(
                    r_co[phase, 1], r_co[phase, 0], g, n - b, 0)

    def send_rims(phase, it, sl):
        def take(ch, row, rows):
            return acc[it, sl, ch, 1, row:row + rows]
        for ch in range(2):
            s_ud[phase, 0, ch] = acc[it, sl, ch, 0, 0:b]
            s_ud[phase, 1, ch] = acc[it, sl, ch, 0, n + b:ext]
        for i, lane in enumerate((n - b, 0)):
            s_lr[phase, i] = pack(take, lane, b, n)
            s_co[phase, i] = pack(take, lane, 0, b)
            s_co[phase, 2 + i] = pack(take, lane, n + b, b)
        send(phase)

    def fold(phase, it, sl):
        wait_recv(phase)
        for ch in range(2):
            for h in range(2):
                g = 2 * ch + h
                row = h * (n // 2)
                core[ch, row:row + n // 2] = acc[it, sl, ch, 0, b + row:b + row + n // 2] + pair(
                    r_lr[phase, 1], r_lr[phase, 0], g, 0, n - b)
            core[ch, 0:b] = core[ch, 0:b] + r_ud[phase, 1, ch]
            core[ch, n - b:n] = core[ch, n - b:n] + r_ud[phase, 0, ch]
            for h in range(2):
                g = 2 * ch + h
                row = h * (b // 2)
                core[ch, row:row + b // 2] = core[ch, row:row + b // 2] + pair(
                    r_co[phase, 3], r_co[phase, 2], g, 0, n - b)
                row = n - b + h * (b // 2)
                core[ch, row:row + b // 2] = core[ch, row:row + b // 2] + pair(
                    r_co[phase, 1], r_co[phase, 0], g, 0, n - b)
        for ch in range(2):
            k = 2 * sl + ch
            new = bord[k, 0, b:b + n] - STEP * core[ch]
            if it == ITERS - 1:
                out[sl, ch] = new
            else:
                bord[k, 0, b:b + n] = new

    def parts(x):
        hi = x.astype(BF)
        return hi, (x - hi.astype(F32)).astype(BF)

    def put_col(s, re, im):
        cols = slice(s * n, (s + 1) * n)
        for i, x in enumerate((re, im)):
            hi, lo = parts(x)
            xc[i * n:(i + 1) * n, cols] = hi
            xc[(2 + i) * n:(3 + i) * n, cols] = lo
            xc[(4 + i) * n:(5 + i) * n, cols] = hi

    def left(t, p):
        cols = slice(2 * p * n, 2 * (p + 1) * n)
        yb[:, cols] = jnp.dot(lefts[t], xc[:, cols], preferred_element_type=F32)

    def right(t, p):
        for s in (2 * p, 2 * p + 1):
            rows = slice(s * n, (s + 1) * n)
            for i in range(2):
                hi, lo = parts(yb[i * n:(i + 1) * n, rows])
                xr[rows, i * n:(i + 1) * n] = hi
                xr[rows, (2 + i) * n:(3 + i) * n] = lo
                xr[rows, (4 + i) * n:(5 + i) * n] = hi
        rows = slice(2 * p * n, 2 * (p + 1) * n)
        zb[rows] = jnp.dot(xr[rows], rights[t], preferred_element_type=F32)

    def result(s):
        return zb[s * n:(s + 1) * n, 0:n], zb[s * n:(s + 1) * n, n:2 * n]

    def window(s, k):
        row, col = offs[0, s], offs[1, s]
        strip = jnp.concatenate([bord[k, h, pl.ds(row, n), :] for h in range(2)], axis=1)
        shift = lax.rem(2 * n + b - col, 2 * n)
        return pltpu.roll(strip, shift, 1)[:, 0:n]

    def place(s, ch, g):
        shift = lax.rem(2 * n - b + offs[1, s], 2 * n)
        wide = jnp.concatenate([g, jnp.zeros_like(g)], axis=1)
        wide = pltpu.roll(wide, shift, 1)
        for h in range(2):
            gpad[s, ch, h, 2 * b:2 * b + n] = wide[:, h * n:(h + 1) * n]

    def gather(it, sl, ranges):
        for ch in range(2):
            for h, row, rows in ranges:
                total = None
                for s in range(slots):
                    start = 2 * b + row - offs[0, s]
                    term = gpad[s, ch, h, pl.ds(start, rows), :]
                    total = term if total is None else total + term
                acc[it, sl, ch, h, row:row + rows] = total

    rims = ((1, 0, ext), (0, 0, b), (0, n + b, b))
    middle = ((0, b, n),)

    def fetch(i):
        pairs = ((obj_h, obj), (probe_h, probe), (lefts_h.at[0], lefts.at[0]),
                 (rights_h.at[0], rights.at[0]), (inten_h.at[0, 0], inten),
                 (lefts_h.at[1:], lefts.at[1:]), (rights_h.at[1:], rights.at[1:]))
        return pltpu.make_async_copy(*pairs[i], in_sem.at[i])

    for i in range(7):
        fetch(i).start()
    barrier = pltpu.get_barrier_semaphore()
    for dr, dc in DIRS:
        @pl.when(exists(dr, dc))
        def _(dr=dr, dc=dc):
            pl.semaphore_signal(barrier, inc=1, device_id=(me_r + dr, me_c + dc),
                                device_id_type=MESH)
    for d, (dr, dc) in enumerate(DIRS):
        @pl.when(jnp.logical_not(exists(-dr, -dc)))
        def _(d=d):
            for phase in range(4 * ITERS):
                dst = bufs(phase, d)[1]
                dst[...] = jnp.zeros(dst.shape, F32)
    for s in range(slots):
        for ch in range(2):
            for h in range(2):
                gpad[s, ch, h, 0:2 * b] = jnp.zeros((2 * b, n), F32)
                gpad[s, ch, h, 2 * b + n:] = jnp.zeros((2 * b, n), F32)
    fetch(0).wait()
    peers = sum(exists(dr, dc).astype(jnp.int32) for dr, dc in DIRS)
    pl.semaphore_wait(barrier, peers)
    for sl in range(2):
        send_halo(sl, lambda ch, row, rows, sl=sl: obj[sl, ch, row:row + rows, :])
    for sl in range(2):
        for ch in range(2):
            bord[2 * sl + ch, 0, b:b + n] = obj[sl, ch]
    for i in range(1, 5):
        fetch(i).wait()
    for s in range(slots):
        amp[s] = jnp.sqrt(inten[s])

    live = counts[0, 0]
    pr, pi = probe.at[0], probe.at[1]

    def both(step):
        def run(p):
            for s in (2 * p, 2 * p + 1):
                step(s)
        return run

    def incident(s):
        ar, ai = window(s, 0), window(s, 1)
        put_col(s, pr[...] * ar - pi[...] * ai, pr[...] * ai + pi[...] * ar)

    def second_windows():
        for s in range(slots):
            win2[s, 0], win2[s, 1] = window(s, 2), window(s, 3)

    def exit_wave(s):
        ur, ui = result(s)
        ar, ai = win2[s, 0], win2[s, 1]
        prop[s, 0], prop[s, 1] = ur, ui
        put_col(s, ur * ar - ui * ai, ur * ai + ui * ar)

    def residual(s):
        fr, fi = result(s)
        scale = 1.0 - amp[s] * lax.rsqrt(fr * fr + fi * fi + 1.0)
        scale = scale * (s < live).astype(F32)
        put_col(s, fr * scale, fi * scale)

    def back_wave(s):
        br, bi = result(s)
        ar, ai = win2[s, 0], win2[s, 1]
        put_col(s, ar * br + ai * bi, ar * bi - ai * br)

    def grad_second(s):
        br, bi = result(s)
        ur, ui = prop[s, 0], prop[s, 1]
        place(s, 0, ur * br + ui * bi)
        place(s, 1, ur * bi - ui * br)

    def grad_first(s):
        br, bi = result(s)
        place(s, 0, pr[...] * br + pi[...] * bi)
        place(s, 1, pr[...] * bi - pi[...] * br)

    def prepare_and_left(prep, t):
        for p in range(slots // 2):
            both(prep)(p)
            left(t, p)

    def all_right(t):
        for p in range(slots // 2):
            right(t, p)

    for it in range(ITERS):
        base = 2 + 4 * it
        last = it == ITERS - 1
        if it:
            recv_halo(base - 2, 1)
            second_windows()
            recv_halo(base - 1, 0)
        else:
            recv_halo(0, 0)
        prepare_and_left(incident, 0)
        if not it:
            recv_halo(1, 1)
            second_windows()
        all_right(0)
        if not it:
            for i in (5, 6):
                fetch(i).wait()
        prepare_and_left(exit_wave, 1)
        all_right(1)
        prepare_and_left(residual, 2)
        all_right(2)
        for p in range(slots // 2):
            both(back_wave)(p)
            left(3, p)
            both(grad_second)(p)
        gather(it, 1, rims)
        send_rims(base, it, 1)
        gather(it, 1, middle)
        all_right(3)
        for p in range(slots // 2):
            both(grad_first)(p)
        gather(it, 0, rims)
        send_rims(base + 1, it, 0)
        gather(it, 0, middle)
        fold(base, it, 1)
        if not last:
            send_halo(base + 2, lambda ch, row, rows: bord[2 + ch, 0, b + row:b + row + rows])
        fold(base + 1, it, 0)
        if not last:
            send_halo(base + 3, lambda ch, row, rows: bord[ch, 0, b + row:b + row + rows])
    for phase in range(4 * ITERS):
        wait_send(phase)


def local(nr, nc, object_field, probe_field, intensity, counts, offsets):
    n = object_field.shape[-1]
    b = BORDER
    slots = intensity.shape[2]
    ext = n + 2 * b
    lefts, rights = tables(n)
    phases = 4 * ITERS
    vmem = pl.BlockSpec(memory_space=pltpu.VMEM)
    hbm = pl.BlockSpec(memory_space=pltpu.HBM)
    smem = pl.BlockSpec(memory_space=pltpu.SMEM)
    messages = [
        pltpu.VMEM((phases, 2, 2, b, n), F32),
        pltpu.VMEM((phases, 2, n // 2, n), F32),
        pltpu.VMEM((phases, 4, b // 2, n), F32),
    ]
    return pl.pallas_call(
        functools.partial(kernel, nr, nc),
        out_shape=jax.ShapeDtypeStruct(object_field.shape, F32),
        in_specs=[hbm, hbm, hbm, smem, smem, hbm, hbm],
        out_specs=vmem,
        scratch_shapes=[
            pltpu.VMEM(object_field.shape, F32),
            pltpu.VMEM(probe_field.shape, F32),
            pltpu.VMEM((slots, n, n), F32),
            pltpu.VMEM(lefts.shape, BF),
            pltpu.VMEM(rights.shape, BF),
            pltpu.SemaphoreType.DMA((7,)),
            pltpu.VMEM((2 * n, slots * n), F32),
            pltpu.VMEM((4, 2, ext, n), F32),
            pltpu.VMEM((slots, n, n), F32),
            pltpu.VMEM((slots, 2, n, n), F32),
            pltpu.VMEM((slots, 2, n, n), F32),
            pltpu.VMEM((6 * n, slots * n), BF),
            pltpu.VMEM((slots * n, 6 * n), BF),
            pltpu.VMEM((slots * n, 2 * n), F32),
            pltpu.VMEM((slots, 2, 2, n + 4 * b, n), F32),
            pltpu.VMEM((ITERS, 2, 2, 2, ext, n), F32),
            pltpu.VMEM((2, n, n), F32),
            *messages,
            *messages,
            pltpu.SemaphoreType.DMA((phases, 8)),
            pltpu.SemaphoreType.DMA((phases, 8)),
        ],
        compiler_params=pltpu.CompilerParams(
            collective_id=0, has_side_effects=True, vmem_limit_bytes=63 * 1024 * 1024),
    )(object_field, probe_field, intensity, counts, jnp.swapaxes(offsets[0, 0], 0, 1),
      jnp.asarray(lefts), jnp.asarray(rights))


def solution(mesh):
    in_specs = (
        P(None, None, "row", "col"),
        P(),
        P("row", "col", None, None, None),
        P("row", "col"),
        P("row", "col", None, None),
    )
    out_specs = P(None, None, "row", "col")
    step = functools.partial(local, mesh.shape["row"], mesh.shape["col"])
    return jax.shard_map(step, mesh=mesh, in_specs=in_specs, out_specs=out_specs, check_vma=False)
```

```python
import functools

import jax
import jax.numpy as jnp
import ml_dtypes
import numpy as np
from jax import lax
from jax.experimental import pallas as pl
from jax.experimental.pallas import tpu as pltpu
from jax.sharding import PartitionSpec as P

BORDER = 32
ITERS = 2
STEP = 0.25
CHIRP = 0.7
DIRS = ((-1, 0), (1, 0), (0, -1), (0, 1), (-1, -1), (-1, 1), (1, -1), (1, 1))
BF = jnp.bfloat16
F32 = jnp.float32
MESH = pl.DeviceIdType.MESH


def tables(n):
    k = np.arange(n)
    ang = -2.0 * np.pi / n * ((k[:, None] * k[None, :]) % n)
    fourier = np.exp(1j * ang) / np.sqrt(n)
    freq = np.where(k < n // 2, k, k - n).astype(np.float64)
    kern = np.exp(-1j * CHIRP * np.pi / n * freq * freq)
    prop = fourier.conj() @ (kern[:, None] * fourier)
    prop = (prop + prop.T) / 2
    out = []
    for m in (prop, fourier):
        for mat in (np.block([[m.real, -m.imag], [m.imag, m.real]]),
                    np.block([[m.real, m.imag], [-m.imag, m.real]])):
            hi = mat.astype(np.float32).astype(ml_dtypes.bfloat16)
            lo = (mat - hi.astype(np.float64)).astype(np.float32).astype(ml_dtypes.bfloat16)
            out.append(np.stack([hi, lo]))
    return np.stack(out)


FACTORS = ((0, 1), (2, 3), (3, 2), (1, 0))


def kernel(nr, nc, obj_h, probe_h, inten_h, counts, offs, tabs_h, out,
           obj, probe, inten, tabs, in_sem, yb, bord, amp, prop, win2, xc, xr, zb, gpad, acc, core,
           s_ud, s_lr, s_co, r_ud, r_lr, r_co, send_sem, recv_sem):
    n = probe.shape[-1]
    b = BORDER
    slots = inten.shape[0]
    ext = n + 2 * b
    me_r, me_c = lax.axis_index("row"), lax.axis_index("col")
    lane_group = lax.broadcasted_iota(jnp.int32, (1, n), 1) // b

    def exists(dr, dc):
        ok = None
        for pos, step, count in ((me_r, dr, nr), (me_c, dc, nc)):
            if step:
                cond = (pos > 0) if step < 0 else (pos < count - 1)
                ok = cond if ok is None else jnp.logical_and(ok, cond)
        return ok

    def bufs(phase, d):
        if d < 2:
            return s_ud.at[phase, d], r_ud.at[phase, d]
        if d < 4:
            return s_lr.at[phase, d - 2], r_lr.at[phase, d - 2]
        return s_co.at[phase, d - 4], r_co.at[phase, d - 4]

    def message(phase, d):
        src, dst = bufs(phase, d)
        dr, dc = DIRS[d]
        return pltpu.make_async_remote_copy(
            src_ref=src, dst_ref=dst,
            send_sem=send_sem.at[phase, d], recv_sem=recv_sem.at[phase, d],
            device_id=(me_r + dr, me_c + dc), device_id_type=MESH)

    def send(phase):
        for d in (2, 3, 4, 5, 6, 7, 0, 1):
            pl.when(exists(*DIRS[d]))(lambda d=d: message(phase, d).start())

    def wait_recv(phase):
        for d, (dr, dc) in enumerate(DIRS):
            pl.when(exists(-dr, -dc))(lambda d=d: message(phase, d).wait_recv())

    def wait_send(phase):
        for d, (dr, dc) in enumerate(DIRS):
            pl.when(exists(dr, dc))(lambda d=d: message(phase, d).wait_send())

    def pack(take, lane0, row0, rows):
        half = rows // 2
        total = None
        for g in range(4):
            piece = take(g // 2, row0 + (g % 2) * half, half)
            shift = (b * g - lane0) % n
            if shift:
                piece = pltpu.roll(piece, shift, 1)
            total = piece if total is None else jnp.where(lane_group == g, piece, total)
        return total

    def unpack(msg, g, lane0):
        shift = (lane0 - b * g) % n
        return pltpu.roll(msg, shift, 1) if shift else msg

    def pair(left_msg, right_msg, g, left_lane, right_lane):
        zero = jnp.zeros_like(left_msg)
        return jnp.where(lane_group == left_lane // b, unpack(left_msg, g, left_lane),
                         jnp.where(lane_group == right_lane // b,
                                   unpack(right_msg, g, right_lane), zero))

    def send_halo(phase, take):
        for ch in range(2):
            s_ud[phase, 0, ch] = take(ch, 0, b)
            s_ud[phase, 1, ch] = take(ch, n - b, b)
        for i, lane in enumerate((0, n - b)):
            s_lr[phase, i] = pack(take, lane, 0, n)
            s_co[phase, i] = pack(take, lane, 0, b)
            s_co[phase, 2 + i] = pack(take, lane, n - b, b)
        send(phase)

    def recv_halo(phase, sl):
        wait_recv(phase)
        for ch in range(2):
            k = 2 * sl + ch
            bord[k, 0, 0:b] = r_ud[phase, 1, ch]
            bord[k, 0, n + b:ext] = r_ud[phase, 0, ch]
            for h in range(2):
                g = 2 * ch + h
                row = b + h * (n // 2)
                bord[k, 1, row:row + n // 2] = pair(
                    r_lr[phase, 1], r_lr[phase, 0], g, n - b, 0)
                row = h * (b // 2)
                bord[k, 1, row:row + b // 2] = pair(
                    r_co[phase, 3], r_co[phase, 2], g, n - b, 0)
                row = n + b + h * (b // 2)
                bord[k, 1, row:row + b // 2] = pair(
                    r_co[phase, 1], r_co[phase, 0], g, n - b, 0)

    def send_rims(phase, it, sl):
        def take(ch, row, rows):
            return acc[it, sl, ch, 1, row:row + rows]
        for ch in range(2):
            s_ud[phase, 0, ch] = acc[it, sl, ch, 0, 0:b]
            s_ud[phase, 1, ch] = acc[it, sl, ch, 0, n + b:ext]
        for i, lane in enumerate((n - b, 0)):
            s_lr[phase, i] = pack(take, lane, b, n)
            s_co[phase, i] = pack(take, lane, 0, b)
            s_co[phase, 2 + i] = pack(take, lane, n + b, b)
        send(phase)

    def fold(phase, it, sl):
        wait_recv(phase)
        for ch in range(2):
            for h in range(2):
                g = 2 * ch + h
                row = h * (n // 2)
                core[ch, row:row + n // 2] = acc[it, sl, ch, 0, b + row:b + row + n // 2] + pair(
                    r_lr[phase, 1], r_lr[phase, 0], g, 0, n - b)
            core[ch, 0:b] = core[ch, 0:b] + r_ud[phase, 1, ch]
            core[ch, n - b:n] = core[ch, n - b:n] + r_ud[phase, 0, ch]
            for h in range(2):
                g = 2 * ch + h
                row = h * (b // 2)
                core[ch, row:row + b // 2] = core[ch, row:row + b // 2] + pair(
                    r_co[phase, 3], r_co[phase, 2], g, 0, n - b)
                row = n - b + h * (b // 2)
                core[ch, row:row + b // 2] = core[ch, row:row + b // 2] + pair(
                    r_co[phase, 1], r_co[phase, 0], g, 0, n - b)
        for ch in range(2):
            k = 2 * sl + ch
            new = bord[k, 0, b:b + n] - STEP * core[ch]
            if it == ITERS - 1:
                out[sl, ch] = new
            else:
                bord[k, 0, b:b + n] = new

    def parts(x):
        hi = x.astype(BF)
        return hi, (x - hi.astype(F32)).astype(BF)

    def put_col(s, re, im):
        cols = slice(s * n, (s + 1) * n)
        for i, x in enumerate((re, im)):
            hi, lo = parts(x)
            xc[i * n:(i + 1) * n, cols] = hi
            xc[(2 + i) * n:(3 + i) * n, cols] = lo

    dot = functools.partial(jnp.dot, preferred_element_type=F32)

    def left(t, p):
        cols = slice(2 * p * n, 2 * (p + 1) * n)
        hi, lo = xc[0:2 * n, cols], xc[2 * n:4 * n, cols]
        m = FACTORS[t][0]
        yb[:, cols] = dot(tabs[m, 0], hi) + (dot(tabs[m, 0], lo) + dot(tabs[m, 1], hi))

    def right(t, p):
        for s in (2 * p, 2 * p + 1):
            rows = slice(s * n, (s + 1) * n)
            for i in range(2):
                hi, lo = parts(yb[i * n:(i + 1) * n, rows])
                xr[rows, i * n:(i + 1) * n] = hi
                xr[rows, (2 + i) * n:(3 + i) * n] = lo
        rows = slice(2 * p * n, 2 * (p + 1) * n)
        hi, lo = xr[rows, 0:2 * n], xr[rows, 2 * n:4 * n]
        m = FACTORS[t][1]
        zb[rows] = dot(hi, tabs[m, 0]) + (dot(lo, tabs[m, 0]) + dot(hi, tabs[m, 1]))

    def result(s):
        return zb[s * n:(s + 1) * n, 0:n], zb[s * n:(s + 1) * n, n:2 * n]

    def window(s, k):
        row, col = offs[0, s], offs[1, s]
        strip = jnp.concatenate([bord[k, h, pl.ds(row, n), :] for h in range(2)], axis=1)
        shift = lax.rem(2 * n + b - col, 2 * n)
        return pltpu.roll(strip, shift, 1)[:, 0:n]

    def place(s, ch, g):
        shift = lax.rem(2 * n - b + offs[1, s], 2 * n)
        wide = jnp.concatenate([g, jnp.zeros_like(g)], axis=1)
        wide = pltpu.roll(wide, shift, 1)
        for h in range(2):
            gpad[s, ch, h, 2 * b:2 * b + n] = wide[:, h * n:(h + 1) * n]

    def gather(it, sl, ranges):
        for ch in range(2):
            for h, row, rows in ranges:
                total = None
                for s in range(slots):
                    start = 2 * b + row - offs[0, s]
                    term = gpad[s, ch, h, pl.ds(start, rows), :]
                    total = term if total is None else total + term
                acc[it, sl, ch, h, row:row + rows] = total

    rims = ((1, 0, ext), (0, 0, b), (0, n + b, b))
    middle = ((0, b, n),)

    def fetch(i):
        pairs = ((obj_h, obj), (probe_h, probe), (tabs_h, tabs), (inten_h.at[0, 0], inten))
        return pltpu.make_async_copy(*pairs[i], in_sem.at[i])

    for i in range(4):
        fetch(i).start()
    barrier = pltpu.get_barrier_semaphore()
    for dr, dc in DIRS:
        @pl.when(exists(dr, dc))
        def _(dr=dr, dc=dc):
            pl.semaphore_signal(barrier, inc=1, device_id=(me_r + dr, me_c + dc),
                                device_id_type=MESH)
    for d, (dr, dc) in enumerate(DIRS):
        @pl.when(jnp.logical_not(exists(-dr, -dc)))
        def _(d=d):
            for phase in range(4 * ITERS):
                dst = bufs(phase, d)[1]
                dst[...] = jnp.zeros(dst.shape, F32)
    for s in range(slots):
        for ch in range(2):
            for h in range(2):
                gpad[s, ch, h, 0:2 * b] = jnp.zeros((2 * b, n), F32)
                gpad[s, ch, h, 2 * b + n:] = jnp.zeros((2 * b, n), F32)
    fetch(0).wait()
    peers = sum(exists(dr, dc).astype(jnp.int32) for dr, dc in DIRS)
    pl.semaphore_wait(barrier, peers)
    for sl in range(2):
        send_halo(sl, lambda ch, row, rows, sl=sl: obj[sl, ch, row:row + rows, :])
    for sl in range(2):
        for ch in range(2):
            bord[2 * sl + ch, 0, b:b + n] = obj[sl, ch]
    for i in range(1, 4):
        fetch(i).wait()
    for s in range(slots):
        amp[s] = jnp.sqrt(inten[s])

    live = counts[0, 0]
    pr, pi = probe.at[0], probe.at[1]

    def both(step):
        def run(p):
            for s in (2 * p, 2 * p + 1):
                step(s)
        return run

    def incident(s):
        ar, ai = window(s, 0), window(s, 1)
        put_col(s, pr[...] * ar - pi[...] * ai, pr[...] * ai + pi[...] * ar)

    def second_windows():
        for s in range(slots):
            win2[s, 0], win2[s, 1] = window(s, 2), window(s, 3)

    def exit_wave(s):
        ur, ui = result(s)
        ar, ai = win2[s, 0], win2[s, 1]
        prop[s, 0], prop[s, 1] = ur, ui
        put_col(s, ur * ar - ui * ai, ur * ai + ui * ar)

    def residual(s):
        fr, fi = result(s)
        scale = 1.0 - amp[s] * lax.rsqrt(fr * fr + fi * fi + 1.0)
        scale = scale * (s < live).astype(F32)
        put_col(s, fr * scale, fi * scale)

    def back_wave(s):
        br, bi = result(s)
        ar, ai = win2[s, 0], win2[s, 1]
        put_col(s, ar * br + ai * bi, ar * bi - ai * br)

    def grad_second(s):
        br, bi = result(s)
        ur, ui = prop[s, 0], prop[s, 1]
        place(s, 0, ur * br + ui * bi)
        place(s, 1, ur * bi - ui * br)

    def grad_first(s):
        br, bi = result(s)
        place(s, 0, pr[...] * br + pi[...] * bi)
        place(s, 1, pr[...] * bi - pi[...] * br)

    def prepare_and_left(prep, t):
        for p in range(slots // 2):
            both(prep)(p)
            left(t, p)

    def all_right(t):
        for p in range(slots // 2):
            right(t, p)

    for it in range(ITERS):
        base = 2 + 4 * it
        last = it == ITERS - 1
        if it:
            recv_halo(base - 2, 1)
            second_windows()
            recv_halo(base - 1, 0)
        else:
            recv_halo(0, 0)
        prepare_and_left(incident, 0)
        if not it:
            recv_halo(1, 1)
            second_windows()
        all_right(0)
        prepare_and_left(exit_wave, 1)
        all_right(1)
        prepare_and_left(residual, 2)
        all_right(2)
        for p in range(slots // 2):
            both(back_wave)(p)
            left(3, p)
            both(grad_second)(p)
        gather(it, 1, rims)
        send_rims(base, it, 1)
        gather(it, 1, middle)
        all_right(3)
        for p in range(slots // 2):
            both(grad_first)(p)
        gather(it, 0, rims)
        send_rims(base + 1, it, 0)
        gather(it, 0, middle)
        fold(base, it, 1)
        if not last:
            send_halo(base + 2, lambda ch, row, rows: bord[2 + ch, 0, b + row:b + row + rows])
        fold(base + 1, it, 0)
        if not last:
            send_halo(base + 3, lambda ch, row, rows: bord[ch, 0, b + row:b + row + rows])
    for phase in range(4 * ITERS):
        wait_send(phase)


def local(nr, nc, object_field, probe_field, intensity, counts, offsets):
    n = object_field.shape[-1]
    b = BORDER
    slots = intensity.shape[2]
    ext = n + 2 * b
    tabs = tables(n)
    phases = 4 * ITERS
    vmem = pl.BlockSpec(memory_space=pltpu.VMEM)
    hbm = pl.BlockSpec(memory_space=pltpu.HBM)
    smem = pl.BlockSpec(memory_space=pltpu.SMEM)
    messages = [
        pltpu.VMEM((phases, 2, 2, b, n), F32),
        pltpu.VMEM((phases, 2, n // 2, n), F32),
        pltpu.VMEM((phases, 4, b // 2, n), F32),
    ]
    return pl.pallas_call(
        functools.partial(kernel, nr, nc),
        out_shape=jax.ShapeDtypeStruct(object_field.shape, F32),
        in_specs=[hbm, hbm, hbm, smem, smem, hbm],
        out_specs=vmem,
        scratch_shapes=[
            pltpu.VMEM(object_field.shape, F32),
            pltpu.VMEM(probe_field.shape, F32),
            pltpu.VMEM((slots, n, n), F32),
            pltpu.VMEM(tabs.shape, BF),
            pltpu.SemaphoreType.DMA((4,)),
            pltpu.VMEM((2 * n, slots * n), F32),
            pltpu.VMEM((4, 2, ext, n), F32),
            pltpu.VMEM((slots, n, n), F32),
            pltpu.VMEM((slots, 2, n, n), F32),
            pltpu.VMEM((slots, 2, n, n), F32),
            pltpu.VMEM((4 * n, slots * n), BF),
            pltpu.VMEM((slots * n, 4 * n), BF),
            pltpu.VMEM((slots * n, 2 * n), F32),
            pltpu.VMEM((slots, 2, 2, n + 4 * b, n), F32),
            pltpu.VMEM((ITERS, 2, 2, 2, ext, n), F32),
            pltpu.VMEM((2, n, n), F32),
            *messages,
            *messages,
            pltpu.SemaphoreType.DMA((phases, 8)),
            pltpu.SemaphoreType.DMA((phases, 8)),
        ],
        compiler_params=pltpu.CompilerParams(
            collective_id=0, has_side_effects=True, vmem_limit_bytes=63 * 1024 * 1024),
    )(object_field, probe_field, intensity, counts, jnp.swapaxes(offsets[0, 0], 0, 1),
      jnp.asarray(tabs))


def solution(mesh):
    in_specs = (
        P(None, None, "row", "col"),
        P(),
        P("row", "col", None, None, None),
        P("row", "col"),
        P("row", "col", None, None),
    )
    out_specs = P(None, None, "row", "col")
    step = functools.partial(local, mesh.shape["row"], mesh.shape["col"])
    return jax.shard_map(step, mesh=mesh, in_specs=in_specs, out_specs=out_specs, check_vma=False)
```

```python
import functools

import jax
import jax.numpy as jnp
import ml_dtypes
import numpy as np
from jax import lax
from jax.experimental import pallas as pl
from jax.experimental.pallas import tpu as pltpu
from jax.sharding import PartitionSpec as P

BORDER = 32
ITERS = 2
STEP = 0.25
CHIRP = 0.7
DIRS = ((-1, 0), (1, 0), (0, -1), (0, 1), (-1, -1), (-1, 1), (1, -1), (1, 1))
BF = jnp.bfloat16
F32 = jnp.float32
MESH = pl.DeviceIdType.MESH


def tables(n):
    k = np.arange(n)
    ang = -2.0 * np.pi / n * ((k[:, None] * k[None, :]) % n)
    fourier = np.exp(1j * ang) / np.sqrt(n)
    freq = np.where(k < n // 2, k, k - n).astype(np.float64)
    kern = np.exp(-1j * CHIRP * np.pi / n * freq * freq)
    prop = fourier.conj() @ (kern[:, None] * fourier)
    prop = (prop + prop.T) / 2
    out = []
    for m in (prop, fourier):
        for mat in (np.block([[m.real, -m.imag], [m.imag, m.real]]),
                    np.block([[m.real, m.imag], [-m.imag, m.real]])):
            hi = mat.astype(np.float32).astype(ml_dtypes.bfloat16)
            lo = (mat - hi.astype(np.float64)).astype(np.float32).astype(ml_dtypes.bfloat16)
            out.append(np.stack([hi, lo]))
    return np.stack(out)


FACTORS = ((0, 1), (2, 3), (3, 2), (1, 0))


def kernel(nr, nc, obj_h, probe_h, inten_h, counts, offs, tabs_h, out,
           obj, probe, inten, tabs, in_sem, bord, amp, prop, win2, xc, xr, zb, gpad, acc, core,
           s_ud, s_lr, s_co, r_ud, r_lr, r_co, send_sem, recv_sem):
    n = probe.shape[-1]
    b = BORDER
    slots = inten.shape[0]
    ext = n + 2 * b
    me_r, me_c = lax.axis_index("row"), lax.axis_index("col")
    lane = lax.broadcasted_iota(jnp.int32, (1, n), 1)
    lane_group = lane // b

    def exists(dr, dc):
        ok = None
        for pos, step, count in ((me_r, dr, nr), (me_c, dc, nc)):
            if step:
                cond = (pos > 0) if step < 0 else (pos < count - 1)
                ok = cond if ok is None else jnp.logical_and(ok, cond)
        return ok

    def bufs(phase, d):
        if d < 2:
            return s_ud.at[phase, d], r_ud.at[phase, d]
        if d < 4:
            return s_lr.at[phase, d - 2], r_lr.at[phase, d - 2]
        return s_co.at[phase, d - 4], r_co.at[phase, d - 4]

    def message(phase, d):
        src, dst = bufs(phase, d)
        dr, dc = DIRS[d]
        return pltpu.make_async_remote_copy(
            src_ref=src, dst_ref=dst,
            send_sem=send_sem.at[phase, d], recv_sem=recv_sem.at[phase, d],
            device_id=(me_r + dr, me_c + dc), device_id_type=MESH)

    def send(phase):
        for d in (2, 3, 4, 5, 6, 7, 0, 1):
            pl.when(exists(*DIRS[d]))(lambda d=d: message(phase, d).start())

    def wait_recv(phase):
        for d, (dr, dc) in enumerate(DIRS):
            pl.when(exists(-dr, -dc))(lambda d=d: message(phase, d).wait_recv())

    def wait_send(phase):
        for d, (dr, dc) in enumerate(DIRS):
            pl.when(exists(dr, dc))(lambda d=d: message(phase, d).wait_send())

    def pack(take, lane0, row0, rows):
        half = rows // 2
        total = None
        for g in range(4):
            piece = take(g // 2, row0 + (g % 2) * half, half)
            shift = (b * g - lane0) % n
            if shift:
                piece = pltpu.roll(piece, shift, 1)
            total = piece if total is None else jnp.where(lane_group == g, piece, total)
        return total

    def unpack(msg, g, lane0):
        shift = (lane0 - b * g) % n
        return pltpu.roll(msg, shift, 1) if shift else msg

    def pair(left_msg, right_msg, g, left_lane, right_lane):
        zero = jnp.zeros_like(left_msg)
        return jnp.where(lane_group == left_lane // b, unpack(left_msg, g, left_lane),
                         jnp.where(lane_group == right_lane // b,
                                   unpack(right_msg, g, right_lane), zero))

    def send_halo(phase, take):
        for ch in range(2):
            s_ud[phase, 0, ch] = take(ch, 0, b)
            s_ud[phase, 1, ch] = take(ch, n - b, b)
        for i, lane in enumerate((0, n - b)):
            s_lr[phase, i] = pack(take, lane, 0, n)
            s_co[phase, i] = pack(take, lane, 0, b)
            s_co[phase, 2 + i] = pack(take, lane, n - b, b)
        send(phase)

    def recv_halo(phase, sl):
        wait_recv(phase)
        for ch in range(2):
            k = 2 * sl + ch
            bord[k, 0, 0:b] = r_ud[phase, 1, ch]
            bord[k, 0, n + b:ext] = r_ud[phase, 0, ch]
            for h in range(2):
                g = 2 * ch + h
                row = b + h * (n // 2)
                bord[k, 1, row:row + n // 2] = pair(
                    r_lr[phase, 1], r_lr[phase, 0], g, n - b, 0)
                row = h * (b // 2)
                bord[k, 1, row:row + b // 2] = pair(
                    r_co[phase, 3], r_co[phase, 2], g, n - b, 0)
                row = n + b + h * (b // 2)
                bord[k, 1, row:row + b // 2] = pair(
                    r_co[phase, 1], r_co[phase, 0], g, n - b, 0)

    def send_rims(phase, it, sl):
        def take(ch, row, rows):
            return acc[it, sl, ch, 1, row:row + rows]
        for ch in range(2):
            s_ud[phase, 0, ch] = acc[it, sl, ch, 0, 0:b]
            s_ud[phase, 1, ch] = acc[it, sl, ch, 0, n + b:ext]
        for i, lane in enumerate((n - b, 0)):
            s_lr[phase, i] = pack(take, lane, b, n)
            s_co[phase, i] = pack(take, lane, 0, b)
            s_co[phase, 2 + i] = pack(take, lane, n + b, b)
        send(phase)

    def fold(phase, it, sl):
        wait_recv(phase)
        for ch in range(2):
            for h in range(2):
                g = 2 * ch + h
                row = h * (n // 2)
                core[ch, row:row + n // 2] = acc[it, sl, ch, 0, b + row:b + row + n // 2] + pair(
                    r_lr[phase, 1], r_lr[phase, 0], g, 0, n - b)
            core[ch, 0:b] = core[ch, 0:b] + r_ud[phase, 1, ch]
            core[ch, n - b:n] = core[ch, n - b:n] + r_ud[phase, 0, ch]
            for h in range(2):
                g = 2 * ch + h
                row = h * (b // 2)
                core[ch, row:row + b // 2] = core[ch, row:row + b // 2] + pair(
                    r_co[phase, 3], r_co[phase, 2], g, 0, n - b)
                row = n - b + h * (b // 2)
                core[ch, row:row + b // 2] = core[ch, row:row + b // 2] + pair(
                    r_co[phase, 1], r_co[phase, 0], g, 0, n - b)
        for ch in range(2):
            k = 2 * sl + ch
            new = bord[k, 0, b:b + n] - STEP * core[ch]
            if it == ITERS - 1:
                out[sl, ch] = new
            else:
                bord[k, 0, b:b + n] = new

    def parts(x):
        hi = x.astype(BF)
        return hi, (x - hi.astype(F32)).astype(BF)

    def put_col(s, re, im):
        cols = slice(s * n, (s + 1) * n)
        for i, x in enumerate((re, im)):
            hi, lo = parts(x)
            xc[i * n:(i + 1) * n, cols] = hi
            xc[(2 + i) * n:(3 + i) * n, cols] = lo

    dot = functools.partial(jnp.dot, preferred_element_type=F32)

    def left(t, p):
        cols = slice(2 * p * n, 2 * (p + 1) * n)
        hi, lo = xc[0:2 * n, cols], xc[2 * n:4 * n, cols]
        m = FACTORS[t][0]
        y = dot(tabs[m, 0], hi) + (dot(tabs[m, 0], lo) + dot(tabs[m, 1], hi))
        for q in range(2):
            rows = slice((2 * p + q) * n, (2 * p + q + 1) * n)
            for i in range(2):
                hi, lo = parts(y[i * n:(i + 1) * n, q * n:(q + 1) * n])
                xr[rows, i * n:(i + 1) * n] = hi
                xr[rows, (2 + i) * n:(3 + i) * n] = lo

    def right(t, p):
        rows = slice(2 * p * n, 2 * (p + 1) * n)
        hi, lo = xr[rows, 0:2 * n], xr[rows, 2 * n:4 * n]
        m = FACTORS[t][1]
        zb[rows] = dot(hi, tabs[m, 0]) + (dot(lo, tabs[m, 0]) + dot(hi, tabs[m, 1]))

    def result(s):
        return zb[s * n:(s + 1) * n, 0:n], zb[s * n:(s + 1) * n, n:2 * n]

    def window(s, k):
        row, col = offs[0, s], offs[1, s]
        shift = lax.rem(n + b - col, n)
        near, far = [pltpu.roll(bord[k, h, pl.ds(row, n), :], shift, 1) for h in range(2)]
        pos = lane + (col - b)
        return jnp.where((pos >= 0) & (pos < n), near, far)

    def place(s, ch, g):
        col = offs[1, s]
        turned = pltpu.roll(g, lax.rem(n + col - b, n), 1)
        pos = lane - (col - b)
        near = (pos >= 0) & (pos < n)
        gpad[s, ch, 0, 2 * b:2 * b + n] = jnp.where(near, turned, 0.0)
        gpad[s, ch, 1, 2 * b:2 * b + n] = jnp.where(near, 0.0, turned)

    def gather(it, sl, ranges):
        for ch in range(2):
            for h, row, rows in ranges:
                total = None
                for s in range(slots):
                    start = 2 * b + row - offs[0, s]
                    term = gpad[s, ch, h, pl.ds(start, rows), :]
                    total = term if total is None else total + term
                acc[it, sl, ch, h, row:row + rows] = total

    rims = ((1, 0, ext), (0, 0, b), (0, n + b, b))
    middle = ((0, b, n),)

    def fetch(i):
        pairs = ((obj_h, obj), (probe_h, probe), (tabs_h, tabs), (inten_h.at[0, 0], inten))
        return pltpu.make_async_copy(*pairs[i], in_sem.at[i])

    for i in range(4):
        fetch(i).start()
    barrier = pltpu.get_barrier_semaphore()
    for dr, dc in DIRS:
        @pl.when(exists(dr, dc))
        def _(dr=dr, dc=dc):
            pl.semaphore_signal(barrier, inc=1, device_id=(me_r + dr, me_c + dc),
                                device_id_type=MESH)
    for d, (dr, dc) in enumerate(DIRS):
        @pl.when(jnp.logical_not(exists(-dr, -dc)))
        def _(d=d):
            for phase in range(4 * ITERS):
                dst = bufs(phase, d)[1]
                dst[...] = jnp.zeros(dst.shape, F32)
    for s in range(slots):
        for ch in range(2):
            for h in range(2):
                gpad[s, ch, h, 0:2 * b] = jnp.zeros((2 * b, n), F32)
                gpad[s, ch, h, 2 * b + n:] = jnp.zeros((2 * b, n), F32)
    fetch(0).wait()
    peers = sum(exists(dr, dc).astype(jnp.int32) for dr, dc in DIRS)
    pl.semaphore_wait(barrier, peers)
    for sl in range(2):
        send_halo(sl, lambda ch, row, rows, sl=sl: obj[sl, ch, row:row + rows, :])
    for sl in range(2):
        for ch in range(2):
            bord[2 * sl + ch, 0, b:b + n] = obj[sl, ch]
    for i in range(1, 4):
        fetch(i).wait()
    for s in range(slots):
        amp[s] = jnp.sqrt(inten[s])

    live = counts[0, 0]
    pr, pi = probe.at[0], probe.at[1]

    def both(step):
        def run(p):
            for s in (2 * p, 2 * p + 1):
                step(s)
        return run

    def incident(s):
        ar, ai = window(s, 0), window(s, 1)
        put_col(s, pr[...] * ar - pi[...] * ai, pr[...] * ai + pi[...] * ar)

    def second_windows():
        for s in range(slots):
            win2[s, 0], win2[s, 1] = window(s, 2), window(s, 3)

    def exit_wave(s):
        ur, ui = result(s)
        ar, ai = win2[s, 0], win2[s, 1]
        prop[s, 0], prop[s, 1] = ur, ui
        put_col(s, ur * ar - ui * ai, ur * ai + ui * ar)

    def residual(s):
        fr, fi = result(s)
        scale = 1.0 - amp[s] * lax.rsqrt(fr * fr + fi * fi + 1.0)
        scale = scale * (s < live).astype(F32)
        put_col(s, fr * scale, fi * scale)

    def back_wave(s):
        br, bi = result(s)
        ar, ai = win2[s, 0], win2[s, 1]
        put_col(s, ar * br + ai * bi, ar * bi - ai * br)

    def grad_second(s):
        br, bi = result(s)
        ur, ui = prop[s, 0], prop[s, 1]
        place(s, 0, ur * br + ui * bi)
        place(s, 1, ur * bi - ui * br)

    def grad_first(s):
        br, bi = result(s)
        place(s, 0, pr[...] * br + pi[...] * bi)
        place(s, 1, pr[...] * bi - pi[...] * br)

    def prepare_and_left(prep, t):
        for p in range(slots // 2):
            both(prep)(p)
            left(t, p)

    def all_right(t):
        for p in range(slots // 2):
            right(t, p)

    for it in range(ITERS):
        base = 2 + 4 * it
        last = it == ITERS - 1
        if it:
            recv_halo(base - 2, 1)
            second_windows()
            recv_halo(base - 1, 0)
        else:
            recv_halo(0, 0)
        prepare_and_left(incident, 0)
        if not it:
            recv_halo(1, 1)
            second_windows()
        all_right(0)
        prepare_and_left(exit_wave, 1)
        all_right(1)
        prepare_and_left(residual, 2)
        all_right(2)
        for p in range(slots // 2):
            both(back_wave)(p)
            left(3, p)
            both(grad_second)(p)
        gather(it, 1, rims)
        send_rims(base, it, 1)
        gather(it, 1, middle)
        all_right(3)
        for p in range(slots // 2):
            both(grad_first)(p)
        gather(it, 0, rims)
        send_rims(base + 1, it, 0)
        gather(it, 0, middle)
        fold(base, it, 1)
        if not last:
            send_halo(base + 2, lambda ch, row, rows: bord[2 + ch, 0, b + row:b + row + rows])
        fold(base + 1, it, 0)
        if not last:
            send_halo(base + 3, lambda ch, row, rows: bord[ch, 0, b + row:b + row + rows])
    for phase in range(4 * ITERS):
        wait_send(phase)


def move(src, dst, sem):
    pieces = [(i, j) for i in range(src.shape[0]) for j in range(src.shape[1])]
    copies = [pltpu.make_async_copy(src.at[i, j], dst.at[i, j], sem.at[i, j]) for i, j in pieces]
    for copy in copies:
        copy.start()
    for copy in copies:
        copy.wait()


def local(nr, nc, object_field, probe_field, intensity, counts, offsets):
    n = object_field.shape[-1]
    b = BORDER
    slots = intensity.shape[2]
    ext = n + 2 * b
    tabs = tables(n)
    phases = 4 * ITERS
    vmem = pl.BlockSpec(memory_space=pltpu.VMEM)
    hbm = pl.BlockSpec(memory_space=pltpu.HBM)
    smem = pl.BlockSpec(memory_space=pltpu.SMEM)
    messages = [
        pltpu.VMEM((phases, 2, 2, b, n), F32),
        pltpu.VMEM((phases, 2, n // 2, n), F32),
        pltpu.VMEM((phases, 4, b // 2, n), F32),
    ]
    updated = pl.pallas_call(
        functools.partial(kernel, nr, nc),
        out_shape=jax.ShapeDtypeStruct(object_field.shape, F32),
        in_specs=[hbm, hbm, hbm, smem, smem, hbm],
        out_specs=vmem,
        scratch_shapes=[
            pltpu.VMEM(object_field.shape, F32),
            pltpu.VMEM(probe_field.shape, F32),
            pltpu.VMEM((slots, n, n), F32),
            pltpu.VMEM(tabs.shape, BF),
            pltpu.SemaphoreType.DMA((4,)),
            pltpu.VMEM((4, 2, ext, n), F32),
            pltpu.VMEM((slots, n, n), F32),
            pltpu.VMEM((slots, 2, n, n), F32),
            pltpu.VMEM((slots, 2, n, n), F32),
            pltpu.VMEM((4 * n, slots * n), BF),
            pltpu.VMEM((slots * n, 4 * n), BF),
            pltpu.VMEM((slots * n, 2 * n), F32),
            pltpu.VMEM((slots, 2, 2, n + 4 * b, n), F32),
            pltpu.VMEM((ITERS, 2, 2, 2, ext, n), F32),
            pltpu.VMEM((2, n, n), F32),
            *messages,
            *messages,
            pltpu.SemaphoreType.DMA((phases, 8)),
            pltpu.SemaphoreType.DMA((phases, 8)),
        ],
        compiler_params=pltpu.CompilerParams(
            collective_id=0, has_side_effects=True, vmem_limit_bytes=63 * 1024 * 1024),
    )(object_field, probe_field, intensity, counts, jnp.swapaxes(offsets[0, 0], 0, 1),
      jnp.asarray(tabs))
    return pl.pallas_call(
        move,
        out_shape=jax.ShapeDtypeStruct(updated.shape, F32),
        in_specs=[hbm],
        out_specs=hbm,
        scratch_shapes=[pltpu.SemaphoreType.DMA(updated.shape[:2])],
        compiler_params=pltpu.CompilerParams(vmem_limit_bytes=63 * 1024 * 1024),
    )(updated)


def solution(mesh):
    in_specs = (
        P(None, None, "row", "col"),
        P(),
        P("row", "col", None, None, None),
        P("row", "col"),
        P("row", "col", None, None),
    )
    out_specs = P(None, None, "row", "col")
    step = functools.partial(local, mesh.shape["row"], mesh.shape["col"])
    return jax.shard_map(step, mesh=mesh, in_specs=in_specs, out_specs=out_specs, check_vma=False)
```

```python
import functools

import jax
import jax.numpy as jnp
import ml_dtypes
import numpy as np
from jax import lax
from jax.experimental import pallas as pl
from jax.experimental.pallas import tpu as pltpu
from jax.sharding import PartitionSpec as P

BORDER = 32
ITERS = 2
STEP = 0.25
CHIRP = 0.7
DIRS = ((-1, 0), (1, 0), (0, -1), (0, 1), (-1, -1), (-1, 1), (1, -1), (1, 1))
BF = jnp.bfloat16
F32 = jnp.float32
MESH = pl.DeviceIdType.MESH


def tables(n):
    k = np.arange(n)
    ang = -2.0 * np.pi / n * ((k[:, None] * k[None, :]) % n)
    fourier = np.exp(1j * ang) / np.sqrt(n)
    freq = np.where(k < n // 2, k, k - n).astype(np.float64)
    kern = np.exp(-1j * CHIRP * np.pi / n * freq * freq)
    prop = fourier.conj() @ (kern[:, None] * fourier)
    prop = (prop + prop.T) / 2
    out = []
    for m in (prop, fourier):
        for mat in (np.block([[m.real, -m.imag], [m.imag, m.real]]),
                    np.block([[m.real, m.imag], [-m.imag, m.real]])):
            hi = mat.astype(np.float32).astype(ml_dtypes.bfloat16)
            lo = (mat - hi.astype(np.float64)).astype(np.float32).astype(ml_dtypes.bfloat16)
            out.append(np.stack([hi, lo]))
    return np.stack(out)


FACTORS = ((0, 1), (2, 3), (3, 2), (1, 0))


def kernel(nr, nc, obj_h, probe_h, inten_h, counts, offs, tabs_h, out,
           obj, probe, inten, tabs, in_sem, bord, amp, prop, win2, xc, xr, zb, gpad, acc, core,
           s_ud, s_lr, s_co, r_ud, r_lr, r_co, send_sem, recv_sem):
    n = probe.shape[-1]
    b = BORDER
    slots = inten.shape[0]
    ext = n + 2 * b
    me_r, me_c = lax.axis_index("row"), lax.axis_index("col")
    lane = lax.broadcasted_iota(jnp.int32, (1, n), 1)
    lane_group = lane // b

    def exists(dr, dc):
        ok = None
        for pos, step, count in ((me_r, dr, nr), (me_c, dc, nc)):
            if step:
                cond = (pos > 0) if step < 0 else (pos < count - 1)
                ok = cond if ok is None else jnp.logical_and(ok, cond)
        return ok

    def bufs(phase, d):
        if d < 2:
            return s_ud.at[phase, d], r_ud.at[phase, d]
        if d < 4:
            return s_lr.at[phase, d - 2], r_lr.at[phase, d - 2]
        return s_co.at[phase, d - 4], r_co.at[phase, d - 4]

    def message(phase, d):
        src, dst = bufs(phase, d)
        dr, dc = DIRS[d]
        return pltpu.make_async_remote_copy(
            src_ref=src, dst_ref=dst,
            send_sem=send_sem.at[phase, d], recv_sem=recv_sem.at[phase, d],
            device_id=(me_r + dr, me_c + dc), device_id_type=MESH)

    def send(phase):
        for d in (2, 3, 4, 5, 6, 7, 0, 1):
            pl.when(exists(*DIRS[d]))(lambda d=d: message(phase, d).start())

    def wait_recv(phase):
        for d, (dr, dc) in enumerate(DIRS):
            pl.when(exists(-dr, -dc))(lambda d=d: message(phase, d).wait_recv())

    def wait_send(phase):
        for d, (dr, dc) in enumerate(DIRS):
            pl.when(exists(dr, dc))(lambda d=d: message(phase, d).wait_send())

    def pack(take, lane0, row0, rows):
        half = rows // 2
        total = None
        for g in range(4):
            piece = take(g // 2, row0 + (g % 2) * half, half)
            shift = (b * g - lane0) % n
            if shift:
                piece = pltpu.roll(piece, shift, 1)
            total = piece if total is None else jnp.where(lane_group == g, piece, total)
        return total

    def unpack(msg, g, lane0):
        shift = (lane0 - b * g) % n
        return pltpu.roll(msg, shift, 1) if shift else msg

    def pair(left_msg, right_msg, g, left_lane, right_lane):
        zero = jnp.zeros_like(left_msg)
        return jnp.where(lane_group == left_lane // b, unpack(left_msg, g, left_lane),
                         jnp.where(lane_group == right_lane // b,
                                   unpack(right_msg, g, right_lane), zero))

    def send_halo(phase, take):
        for ch in range(2):
            s_ud[phase, 0, ch] = take(ch, 0, b)
            s_ud[phase, 1, ch] = take(ch, n - b, b)
        for i, lane in enumerate((0, n - b)):
            s_lr[phase, i] = pack(take, lane, 0, n)
            s_co[phase, i] = pack(take, lane, 0, b)
            s_co[phase, 2 + i] = pack(take, lane, n - b, b)
        send(phase)

    def recv_halo(phase, sl):
        wait_recv(phase)
        for ch in range(2):
            k = 2 * sl + ch
            bord[k, 0, 0:b] = r_ud[phase, 1, ch]
            bord[k, 0, n + b:ext] = r_ud[phase, 0, ch]
            for h in range(2):
                g = 2 * ch + h
                row = b + h * (n // 2)
                bord[k, 1, row:row + n // 2] = pair(
                    r_lr[phase, 1], r_lr[phase, 0], g, n - b, 0)
                row = h * (b // 2)
                bord[k, 1, row:row + b // 2] = pair(
                    r_co[phase, 3], r_co[phase, 2], g, n - b, 0)
                row = n + b + h * (b // 2)
                bord[k, 1, row:row + b // 2] = pair(
                    r_co[phase, 1], r_co[phase, 0], g, n - b, 0)

    def send_rims(phase, it, sl):
        def take(ch, row, rows):
            return acc[it, sl, ch, 1, row:row + rows]
        for ch in range(2):
            s_ud[phase, 0, ch] = acc[it, sl, ch, 0, 0:b]
            s_ud[phase, 1, ch] = acc[it, sl, ch, 0, n + b:ext]
        for i, lane in enumerate((n - b, 0)):
            s_lr[phase, i] = pack(take, lane, b, n)
            s_co[phase, i] = pack(take, lane, 0, b)
            s_co[phase, 2 + i] = pack(take, lane, n + b, b)
        send(phase)

    def fold(phase, it, sl):
        wait_recv(phase)
        for ch in range(2):
            for h in range(2):
                g = 2 * ch + h
                row = h * (n // 2)
                core[ch, row:row + n // 2] = acc[it, sl, ch, 0, b + row:b + row + n // 2] + pair(
                    r_lr[phase, 1], r_lr[phase, 0], g, 0, n - b)
            core[ch, 0:b] = core[ch, 0:b] + r_ud[phase, 1, ch]
            core[ch, n - b:n] = core[ch, n - b:n] + r_ud[phase, 0, ch]
            for h in range(2):
                g = 2 * ch + h
                row = h * (b // 2)
                core[ch, row:row + b // 2] = core[ch, row:row + b // 2] + pair(
                    r_co[phase, 3], r_co[phase, 2], g, 0, n - b)
                row = n - b + h * (b // 2)
                core[ch, row:row + b // 2] = core[ch, row:row + b // 2] + pair(
                    r_co[phase, 1], r_co[phase, 0], g, 0, n - b)
        for ch in range(2):
            k = 2 * sl + ch
            new = bord[k, 0, b:b + n] - STEP * core[ch]
            if it == ITERS - 1:
                out[sl, ch] = new
            else:
                bord[k, 0, b:b + n] = new

    def parts(x):
        hi = x.astype(BF)
        return hi, (x - hi.astype(F32)).astype(BF)

    def put_col(s, re, im):
        cols = slice(s * n, (s + 1) * n)
        for i, x in enumerate((re, im)):
            hi, lo = parts(x)
            xc[i * n:(i + 1) * n, cols] = hi
            xc[(2 + i) * n:(3 + i) * n, cols] = lo

    dot = functools.partial(jnp.dot, preferred_element_type=F32)

    def left(t, p):
        cols = slice(2 * p * n, 2 * (p + 1) * n)
        hi, lo = xc[0:2 * n, cols], xc[2 * n:4 * n, cols]
        m = FACTORS[t][0]
        y = dot(jnp.concatenate([tabs[m, 0], tabs[m, 0], tabs[m, 1]], axis=1),
                jnp.concatenate([hi, lo, hi], axis=0))
        for q in range(2):
            rows = slice((2 * p + q) * n, (2 * p + q + 1) * n)
            for i in range(2):
                hi, lo = parts(y[i * n:(i + 1) * n, q * n:(q + 1) * n])
                xr[rows, i * n:(i + 1) * n] = hi
                xr[rows, (2 + i) * n:(3 + i) * n] = lo

    def right(t, p):
        rows = slice(2 * p * n, 2 * (p + 1) * n)
        hi, lo = xr[rows, 0:2 * n], xr[rows, 2 * n:4 * n]
        m = FACTORS[t][1]
        zb[rows] = dot(jnp.concatenate([hi, lo, hi], axis=1),
                       jnp.concatenate([tabs[m, 0], tabs[m, 0], tabs[m, 1]], axis=0))

    def result(s):
        return zb[s * n:(s + 1) * n, 0:n], zb[s * n:(s + 1) * n, n:2 * n]

    def window(s, k):
        row, col = offs[0, s], offs[1, s]
        shift = lax.rem(n + b - col, n)
        near, far = [pltpu.roll(bord[k, h, pl.ds(row, n), :], shift, 1) for h in range(2)]
        pos = lane + (col - b)
        return jnp.where((pos >= 0) & (pos < n), near, far)

    def place(s, ch, g):
        col = offs[1, s]
        turned = pltpu.roll(g, lax.rem(n + col - b, n), 1)
        pos = lane - (col - b)
        near = (pos >= 0) & (pos < n)
        gpad[s, ch, 0, 2 * b:2 * b + n] = jnp.where(near, turned, 0.0)
        gpad[s, ch, 1, 2 * b:2 * b + n] = jnp.where(near, 0.0, turned)

    def gather(it, sl, ranges):
        for ch in range(2):
            for h, row, rows in ranges:
                total = None
                for s in range(slots):
                    start = 2 * b + row - offs[0, s]
                    term = gpad[s, ch, h, pl.ds(start, rows), :]
                    total = term if total is None else total + term
                acc[it, sl, ch, h, row:row + rows] = total

    rims = ((1, 0, ext), (0, 0, b), (0, n + b, b))
    middle = ((0, b, n),)

    def fetch(i):
        pairs = ((obj_h, obj), (probe_h, probe), (tabs_h, tabs), (inten_h.at[0, 0], inten))
        return pltpu.make_async_copy(*pairs[i], in_sem.at[i])

    for i in range(4):
        fetch(i).start()
    barrier = pltpu.get_barrier_semaphore()
    for dr, dc in DIRS:
        @pl.when(exists(dr, dc))
        def _(dr=dr, dc=dc):
            pl.semaphore_signal(barrier, inc=1, device_id=(me_r + dr, me_c + dc),
                                device_id_type=MESH)
    for d, (dr, dc) in enumerate(DIRS):
        @pl.when(jnp.logical_not(exists(-dr, -dc)))
        def _(d=d):
            for phase in range(4 * ITERS):
                dst = bufs(phase, d)[1]
                dst[...] = jnp.zeros(dst.shape, F32)
    for s in range(slots):
        for ch in range(2):
            for h in range(2):
                gpad[s, ch, h, 0:2 * b] = jnp.zeros((2 * b, n), F32)
                gpad[s, ch, h, 2 * b + n:] = jnp.zeros((2 * b, n), F32)
    fetch(0).wait()
    peers = sum(exists(dr, dc).astype(jnp.int32) for dr, dc in DIRS)
    pl.semaphore_wait(barrier, peers)
    for sl in range(2):
        send_halo(sl, lambda ch, row, rows, sl=sl: obj[sl, ch, row:row + rows, :])
    for sl in range(2):
        for ch in range(2):
            bord[2 * sl + ch, 0, b:b + n] = obj[sl, ch]
    for i in range(1, 4):
        fetch(i).wait()
    for s in range(slots):
        amp[s] = jnp.sqrt(inten[s])

    live = counts[0, 0]
    pr, pi = probe.at[0], probe.at[1]

    def both(step):
        def run(p):
            for s in (2 * p, 2 * p + 1):
                step(s)
        return run

    def incident(s):
        ar, ai = window(s, 0), window(s, 1)
        put_col(s, pr[...] * ar - pi[...] * ai, pr[...] * ai + pi[...] * ar)

    def second_windows():
        for s in range(slots):
            win2[s, 0], win2[s, 1] = window(s, 2), window(s, 3)

    def exit_wave(s):
        ur, ui = result(s)
        ar, ai = win2[s, 0], win2[s, 1]
        prop[s, 0], prop[s, 1] = ur, ui
        put_col(s, ur * ar - ui * ai, ur * ai + ui * ar)

    def residual(s):
        fr, fi = result(s)
        scale = 1.0 - amp[s] * lax.rsqrt(fr * fr + fi * fi + 1.0)
        scale = scale * (s < live).astype(F32)
        put_col(s, fr * scale, fi * scale)

    def back_wave(s):
        br, bi = result(s)
        ar, ai = win2[s, 0], win2[s, 1]
        put_col(s, ar * br + ai * bi, ar * bi - ai * br)

    def grad_second(s):
        br, bi = result(s)
        ur, ui = prop[s, 0], prop[s, 1]
        place(s, 0, ur * br + ui * bi)
        place(s, 1, ur * bi - ui * br)

    def grad_first(s):
        br, bi = result(s)
        place(s, 0, pr[...] * br + pi[...] * bi)
        place(s, 1, pr[...] * bi - pi[...] * br)

    def prepare_and_left(prep, t):
        for p in range(slots // 2):
            both(prep)(p)
            left(t, p)

    def all_right(t):
        for p in range(slots // 2):
            right(t, p)

    for it in range(ITERS):
        base = 2 + 4 * it
        last = it == ITERS - 1
        if it:
            recv_halo(base - 2, 1)
            second_windows()
            recv_halo(base - 1, 0)
        else:
            recv_halo(0, 0)
        prepare_and_left(incident, 0)
        if not it:
            recv_halo(1, 1)
            second_windows()
        all_right(0)
        prepare_and_left(exit_wave, 1)
        all_right(1)
        prepare_and_left(residual, 2)
        all_right(2)
        for p in range(slots // 2):
            both(back_wave)(p)
            left(3, p)
            both(grad_second)(p)
        gather(it, 1, rims)
        send_rims(base, it, 1)
        gather(it, 1, middle)
        all_right(3)
        for p in range(slots // 2):
            both(grad_first)(p)
        gather(it, 0, rims)
        send_rims(base + 1, it, 0)
        gather(it, 0, middle)
        fold(base, it, 1)
        if not last:
            send_halo(base + 2, lambda ch, row, rows: bord[2 + ch, 0, b + row:b + row + rows])
        fold(base + 1, it, 0)
        if not last:
            send_halo(base + 3, lambda ch, row, rows: bord[ch, 0, b + row:b + row + rows])
    for phase in range(4 * ITERS):
        wait_send(phase)


def local(nr, nc, object_field, probe_field, intensity, counts, offsets):
    n = object_field.shape[-1]
    b = BORDER
    slots = intensity.shape[2]
    ext = n + 2 * b
    tabs = tables(n)
    phases = 4 * ITERS
    vmem = pl.BlockSpec(memory_space=pltpu.VMEM)
    hbm = pl.BlockSpec(memory_space=pltpu.HBM)
    smem = pl.BlockSpec(memory_space=pltpu.SMEM)
    messages = [
        pltpu.VMEM((phases, 2, 2, b, n), F32),
        pltpu.VMEM((phases, 2, n // 2, n), F32),
        pltpu.VMEM((phases, 4, b // 2, n), F32),
    ]
    return pl.pallas_call(
        functools.partial(kernel, nr, nc),
        out_shape=jax.ShapeDtypeStruct(object_field.shape, F32),
        in_specs=[hbm, hbm, hbm, smem, smem, hbm],
        out_specs=vmem,
        scratch_shapes=[
            pltpu.VMEM(object_field.shape, F32),
            pltpu.VMEM(probe_field.shape, F32),
            pltpu.VMEM((slots, n, n), F32),
            pltpu.VMEM(tabs.shape, BF),
            pltpu.SemaphoreType.DMA((4,)),
            pltpu.VMEM((4, 2, ext, n), F32),
            pltpu.VMEM((slots, n, n), F32),
            pltpu.VMEM((slots, 2, n, n), F32),
            pltpu.VMEM((slots, 2, n, n), F32),
            pltpu.VMEM((4 * n, slots * n), BF),
            pltpu.VMEM((slots * n, 4 * n), BF),
            pltpu.VMEM((slots * n, 2 * n), F32),
            pltpu.VMEM((slots, 2, 2, n + 4 * b, n), F32),
            pltpu.VMEM((ITERS, 2, 2, 2, ext, n), F32),
            pltpu.VMEM((2, n, n), F32),
            *messages,
            *messages,
            pltpu.SemaphoreType.DMA((phases, 8)),
            pltpu.SemaphoreType.DMA((phases, 8)),
        ],
        compiler_params=pltpu.CompilerParams(
            collective_id=0, has_side_effects=True, vmem_limit_bytes=63 * 1024 * 1024),
    )(object_field, probe_field, intensity, counts, jnp.swapaxes(offsets[0, 0], 0, 1),
      jnp.asarray(tabs))


def solution(mesh):
    in_specs = (
        P(None, None, "row", "col"),
        P(),
        P("row", "col", None, None, None),
        P("row", "col"),
        P("row", "col", None, None),
    )
    out_specs = P(None, None, "row", "col")
    step = functools.partial(local, mesh.shape["row"], mesh.shape["col"])
    return jax.shard_map(step, mesh=mesh, in_specs=in_specs, out_specs=out_specs, check_vma=False)
```
